256 devices in a mesh: dp: 32 (over z_lo, x, y), tensor: 8 (over z_hi, core).
Axes of the slice: x: 4, y: 4, z: 8 (z_hi: 4, z_lo: 2; z = z_hi * 2 + z_lo), core: 2. Of those that a mesh axis runs over, the one named last changes fastest.
Arguments:
- teacher_hidden: bfloat16 [32768, 6400], P('dp', 'tensor'), may hold values from -6 to 6
- down_weight: bfloat16 [6400, 3200], P('tensor'), may hold values from -0.109375 to 0.109375
- teacher_resid: bfloat16 [32768, 3200], P('dp', 'tensor'), may hold values from -6 to 6
- layer_scale: float32 [3200], replicated, may hold values from 0.3 to 3
- student_x: bfloat16 [32768, 1024], P(('dp', 'tensor')), may hold values from -0.3125 to 0.3125
- norm_gain: float32 [1024], replicated, may hold values from 0.5 to 1.5
- head_weight: bfloat16 [1024, 3200], P(None, 'tensor'), may hold values from -0.1875 to 0.1875
Outputs:
- token_loss: float32 [32768], P(('dp', 'tensor'))
- input_grad: bfloat16 [32768, 1024], P(('dp', 'tensor'))
- head_grad: bfloat16 [1024, 3200], P('dp', 'tensor')
The draws below stay inside these ranges and needn't reach their ends.
All inputs are finite; a program needn't handle non-finite values.
Results may differ from the reference program's by a relative error of at most 0.02.
Values may be sent and summed in bfloat16 or wider, within the bound.
A program may use at most 128 MiB of HBM per device.

```python
import math
import jax
import jax.numpy as jnp
from jax import lax

DT = 3200
FFW = 6400
DS = 1024
TOKENS = 32768
N_TENSOR = 8


def strengthened(values, stream_key, source, target, blocks, factor):
    def block_of(position):
        return (jnp.arange(values.shape[position]) // (values.shape[position] // blocks)).reshape((-1,) + (1,) * (values.ndim - 1 - position))

    first = jax.random.permutation(stream_key, blocks)[block_of(target)]
    second = (block_of(target) + blocks // 2) % blocks
    return jnp.where((block_of(source) == first) | (block_of(source) == second), factor * values, values)


def steps_of(own_key, shape, shards, least, high):
    def one(axis_at, shards_of):
        steps = jax.random.uniform(jax.random.fold_in(jax.random.fold_in(own_key, 6), axis_at), (shards_of,), jnp.float32, least / len(shards), high / len(shards))
        return jnp.repeat(jnp.exp(steps), shape[axis_at] // shards_of).reshape((-1,) + (1,) * (len(shape) - axis_at - 1))

    gain = one(*shards[0])
    for cut in shards[1:]:
        gain = gain * one(*cut)
    return gain


def centred(own_key, dims, scale, limit, split=(), kind=jnp.bfloat16):
    array = jax.random.normal(own_key, dims, jnp.float32) * scale
    if len(split) > 0:
        array = steps_of(own_key, dims, split, -0.22, 0.18) * array
    return jnp.clip(array, min=-limit, max=limit).astype(kind)


def bell_draw_with(rng, shape, deviation, limit, shards, heavy, kind=jnp.bfloat16):
    values = deviation * jax.random.normal(rng, shape, jnp.float32)
    if shards:
        values = values * steps_of(rng, shape, shards, -0.22, 0.18)
    return jnp.clip(strengthened(values, jax.random.fold_in(rng, 3), *heavy), -limit, limit).astype(kind)


def setup_inputs(seed: int = 0) -> dict:
    key_of = jax.random.split(jax.random.key(seed), 8)
    teacher_hidden = centred(key_of[0], (TOKENS, FFW), 1.0, 6.0, ((0, 32), (1, 8)))
    down_weight = bell_draw_with(key_of[1], (FFW, DT), FFW ** -0.5, 0.109375, ((0, 8),), (0, 1, 8, 2.0))
    teacher_resid = centred(key_of[2], (TOKENS, DT), 1.0, 6.0, ((0, 32), (1, 8)))
    layer_scale = jnp.clip(jnp.exp(jax.random.uniform(key_of[3], (DT,), jnp.float32, math.log(0.3), math.log(3.0))), 0.3, 3.0)
    student_x = centred(key_of[4], (TOKENS, DS), 0.05, 0.3125, ((0, 256),))
    norm_gain = jnp.clip(jax.random.uniform(key_of[5], (DS,), jnp.float32, 0.5, 1.5), 0.5, 1.5)
    head_weight = centred(key_of[6], (DS, DT), DS ** -0.5, 0.1875, ((1, 8),))
    return {"teacher_hidden": teacher_hidden, "down_weight": down_weight, "teacher_resid": teacher_resid, "layer_scale": layer_scale, "student_x": student_x, "norm_gain": norm_gain, "head_weight": head_weight}


epsilon = 1e-06

def reference(teacher_hidden, down_weight, teacher_resid, layer_scale, student_x, norm_gain, head_weight):
    token_total = teacher_hidden.shape[0]
    block_width = FFW // N_TENSOR

    def accumulate(running, block_index):
        first_unit = (block_index * block_width).astype(jnp.int32)
        hidden_part = lax.dynamic_slice_in_dim(teacher_hidden, first_unit, block_width, 1)
        weight_part = lax.dynamic_slice_in_dim(down_weight, first_unit, block_width, 0)
        block_sum = jnp.dot(hidden_part, weight_part, preferred_element_type=jnp.float32)
        rounded = lax.optimization_barrier(block_sum.astype(jnp.bfloat16))
        return (running + rounded.astype(jnp.float32), None)
    teacher_sum, _ = lax.scan(accumulate, jnp.zeros((token_total, DT), jnp.float32), jnp.arange(N_TENSOR, dtype=jnp.int32))
    teacher_feat = (teacher_resid.astype(jnp.float32) + layer_scale.astype(jnp.float32) * teacher_sum).astype(jnp.bfloat16)
    values = student_x.astype(jnp.float32)
    centered = values - lax.optimization_barrier(jnp.mean(values, axis=1, keepdims=True))
    inverse = lax.rsqrt(lax.optimization_barrier(jnp.mean(centered * centered, axis=1, keepdims=True)) + epsilon)
    normed = centered * inverse
    normed_out = (normed * norm_gain.astype(jnp.float32)).astype(jnp.bfloat16)
    predicted = jnp.dot(normed_out, head_weight, preferred_element_type=jnp.float32)
    target_wide = teacher_feat.astype(jnp.float32)
    inner_sum = lax.optimization_barrier(jnp.sum(predicted * target_wide, axis=1))
    pred_sq = lax.optimization_barrier(jnp.sum(predicted * predicted, axis=1))
    target_sq = lax.optimization_barrier(jnp.sum(target_wide * target_wide, axis=1))
    scaling = lax.rsqrt((pred_sq + epsilon) * (target_sq + epsilon))
    cosine = inner_sum * scaling
    token_loss = 1.0 - cosine
    pred_grad = ((cosine / (pred_sq + epsilon))[:, None] * predicted - scaling[:, None] * target_wide).astype(jnp.bfloat16)
    head_grad = lax.dot_general(normed_out, pred_grad, (((0,), (0,)), ((), ())), preferred_element_type=jnp.float32)
    back_grad = lax.dot_general(pred_grad, head_weight, (((1,), (1,)), ((), ())), preferred_element_type=jnp.float32)
    normed_grad = back_grad * norm_gain.astype(jnp.float32)
    input_grad = inverse * (normed_grad - lax.optimization_barrier(jnp.mean(normed_grad, axis=1, keepdims=True)) - normed * lax.optimization_barrier(jnp.mean(normed_grad * normed, axis=1, keepdims=True)))
    return (token_loss, input_grad.astype(jnp.bfloat16), head_grad.astype(jnp.bfloat16))
```

```python
import jax
import jax.numpy as jnp
from jax import lax
from jax.sharding import PartitionSpec as P

epsilon = 1e-06


def normalize(student_x, norm_gain):
    values = student_x.astype(jnp.float32)
    centered = values - jnp.mean(values, axis=1, keepdims=True)
    inverse = lax.rsqrt(jnp.mean(centered * centered, axis=1, keepdims=True) + epsilon)
    normed = centered * inverse
    normed_out = (normed * norm_gain).astype(jnp.bfloat16)
    return (normed, inverse, normed_out)


def norm_backward(back_grad, normed, inverse, norm_gain):
    normed_grad = back_grad * norm_gain
    return inverse * (
        normed_grad
        - jnp.mean(normed_grad, axis=1, keepdims=True)
        - normed * jnp.mean(normed_grad * normed, axis=1, keepdims=True)
    )


def cosine_parts(predicted, target_wide, inner_sum, pred_sq, target_sq):
    scaling = lax.rsqrt((pred_sq + epsilon) * (target_sq + epsilon))
    cosine = inner_sum * scaling
    pred_grad = (
        (cosine / (pred_sq + epsilon))[:, None] * predicted - scaling[:, None] * target_wide
    ).astype(jnp.bfloat16)
    return (1.0 - cosine, pred_grad)


def teacher_columns(teacher_hidden, down_weight, teacher_resid, layer_scale):
    column_count = teacher_resid.shape[1]
    first_column = lax.axis_index("tensor") * column_count
    partial_sum = jnp.dot(teacher_hidden, down_weight, preferred_element_type=jnp.float32)
    summed = lax.psum_scatter(
        partial_sum.astype(jnp.bfloat16), "tensor", scatter_dimension=1, tiled=True
    ).astype(jnp.float32)
    scale_part = lax.dynamic_slice_in_dim(layer_scale, first_column, column_count)
    return (teacher_resid.astype(jnp.float32) + scale_part * summed).astype(jnp.bfloat16)


def shards(
    teacher_hidden, down_weight, teacher_resid, layer_scale, student_x, norm_gain, head_weight
):
    own_tokens = student_x.shape[0]
    group_x = lax.all_gather(student_x, "tensor", axis=0, tiled=True)
    _, _, group_out = normalize(group_x, norm_gain)
    normed, inverse, _ = normalize(student_x, norm_gain)
    predicted = jnp.dot(group_out, head_weight, preferred_element_type=jnp.float32)
    target = teacher_columns(teacher_hidden, down_weight, teacher_resid, layer_scale)
    target_wide = target.astype(jnp.float32)
    stats = lax.psum(
        jnp.stack(
            [
                jnp.sum(predicted * target_wide, axis=1),
                jnp.sum(predicted * predicted, axis=1),
                jnp.sum(target_wide * target_wide, axis=1),
            ]
        ),
        "tensor",
    )
    losses, pred_grad = cosine_parts(predicted, target_wide, stats[0], stats[1], stats[2])
    losses = lax.dynamic_slice_in_dim(losses, lax.axis_index("tensor") * own_tokens, own_tokens)
    back_part = lax.dot_general(
        pred_grad, head_weight, (((1,), (1,)), ((), ())), preferred_element_type=jnp.float32
    )
    back_grad = lax.psum_scatter(
        back_part.astype(jnp.bfloat16), "tensor", scatter_dimension=0, tiled=True
    ).astype(jnp.float32)
    grad_block = lax.dot_general(
        group_out, pred_grad, (((0,), (0,)), ((), ())), preferred_element_type=jnp.float32
    )
    head_grad = lax.psum_scatter(grad_block, "dp", scatter_dimension=0, tiled=True).astype(
        jnp.bfloat16
    )
    input_grad = norm_backward(back_grad, normed, inverse, norm_gain).astype(jnp.bfloat16)
    return (losses, input_grad, head_grad)


def solution(mesh):
    placed = (
        P("dp", "tensor"),
        P("tensor", None),
        P("dp", "tensor"),
        P(),
        P(("dp", "tensor"), None),
        P(),
        P(None, "tensor"),
    )
    return jax.shard_map(
        shards,
        mesh=mesh,
        in_specs=placed,
        out_specs=(P(("dp", "tensor")), P(("dp", "tensor"), None), P("dp", "tensor")),
        check_vma=False,
    )
```

```python
import functools

import jax
import jax.numpy as jnp
from jax import lax
from jax.experimental import pallas as pl
from jax.experimental.pallas import tpu as pltpu
from jax.sharding import PartitionSpec as P

MESH = pl.DeviceIdType.MESH
F32 = jnp.float32
BF16 = jnp.bfloat16
epsilon = 1e-06

DT = 3200
HALF = 1664
STEP = 1536
WIDE = 512
OUTW = 896
CH = 2


def wide(value):
    return value.astype(F32)


def kernel(
    hid_hbm, w_hbm, res_hbm, ls_ref, x_hbm, gain_ref, head_hbm,
    loss_ref, igrad_ref, hgrad_ref,
    hid, w, res, hrow, part, cs, cr, zs, ra, rb, fa, fb, hw, hd, xs, nb, nt, pr, pg,
    st, sr, bp, br, gs, r1, f1, s1, r2, s2, rz, hgs,
    lsem, ssem, rsem,
):
    d = lax.axis_index("dp")
    t = lax.axis_index("tensor")
    zl, x, y = d // 16, (d // 4) % 4, d % 4
    p, c = t // 2, t % 2
    p1, p2, p3 = p + 1 - 2 * (p % 2), (p + 2) % 4, 3 - p
    peer = 1 - c

    def at(zl=zl, x=x, y=y, p=p, c=c):
        return {"dp": zl * 16 + x * 4 + y, "tensor": p * 2 + c}

    counts = [0]

    def ids(n):
        first = counts[0]
        counts[0] += n
        return first

    def remote(src, dst, j, device):
        return pltpu.make_async_remote_copy(
            src_ref=src, dst_ref=dst, send_sem=ssem.at[j], recv_sem=rsem.at[j],
            device_id=device, device_id_type=MESH,
        )

    row_block = x * 4 + y
    loads = [
        pltpu.make_async_copy(
            head_hbm.at[pl.ds(pl.multiple_of(row_block * 64, 64), 64)], hrow, lsem.at[0]
        ),
        pltpu.make_async_copy(x_hbm, xs.at[c], lsem.at[1]),
        pltpu.make_async_copy(w_hbm, w, lsem.at[2]),
        pltpu.make_async_copy(hid_hbm, hid, lsem.at[3]),
        pltpu.make_async_copy(res_hbm, res, lsem.at[4]),
    ]
    for load in loads:
        load.start()

    barrier = pltpu.get_barrier_semaphore()
    zz = p * 2 + zl
    greeted = [at(c=peer)]
    for o in range(1, 8):
        other = (zz + o) % 8
        greeted.append(at(zl=other % 2, p=other // 2))
    for o in range(1, 4):
        greeted.append(at(x=(x + o) % 4))
        greeted.append(at(y=(y + o) % 4))
    for device in greeted:
        pl.semaphore_signal(barrier, inc=1, device_id=device, device_id_type=MESH)

    spot = lax.broadcasted_iota(jnp.int32, (400, WIDE), 1)
    sel = (spot == lax.broadcasted_iota(jnp.int32, (400, WIDE), 0) + 16 * t).astype(BF16)
    hw[0] = jnp.zeros((64, WIDE), BF16)
    hw[9] = jnp.zeros((64, WIDE), BF16)
    loads[0].wait()
    hw[1 + t] = jnp.dot(hrow[...], sel, preferred_element_type=F32).astype(BF16)

    pl.semaphore_wait(barrier, len(greeted))

    x_id = ids(1)

    def x_copy():
        return remote(xs.at[c], xs.at[c], x_id, at(c=peer))

    loads[1].wait()
    x_copy().start()

    hz_id = ids(3)

    def hz_copy(o):
        return remote(hw.at[1 + t], hw.at[1 + t], hz_id + o - 1, at(p=(p + o) % 4))

    for o in (1, 3, 2):
        hz_copy(o).start()

    hc_id = ids(4)

    def hc_copy(o):
        slot = 1 + 2 * ((p + 4 - o) % 4) + c
        return remote(hw.at[slot], hw.at[slot], hc_id + o, at(c=peer))

    h1_id = ids(6)

    def h1_copy(m, o):
        block = hd.at[x, y, :, pl.ds(896 * m, 896 - 128 * m)]
        device = at(x=(x + o) % 4) if m == 0 else at(y=(y + o) % 4)
        return remote(block, block, h1_id + 3 * m + o - 1, device)

    h2_id = ids(6)

    def h2_copy(m, o):
        if m == 0:
            block, device = hd.at[:, y, :, pl.ds(0, 896)], at(y=(y + o) % 4)
        else:
            block, device = hd.at[x, :, :, pl.ds(896, 768)], at(x=(x + o) % 4)
        return remote(block, block, h2_id + 3 * m + o - 1, device)

    def head_first():
        for o in range(4):
            if o:
                hz_copy(o).wait_recv()
            hc_copy(o).start()
        for o in range(4):
            hc_copy(o).wait_recv()
        for j in range(13):
            tile = hw[1 + 4 * c + j // 3, :, (j % 3) * 128 : (j % 3) * 128 + 128]
            if j % 3 == 0:
                tile = tile + hw[4 * c + j // 3, :, 384:512]
            hd[x, y, :, j * 128 : (j + 1) * 128] = tile
        for o in (1, 3, 2):
            for m in range(2):
                h1_copy(m, o).start()

    def head_second():
        for o in range(1, 4):
            for m in range(2):
                h1_copy(m, o).wait_recv()
        for o in (1, 3, 2):
            for m in range(2):
                h2_copy(m, o).start()

    core_id = ids(4)

    def core_copy(k):
        return remote(cs.at[k], cr.at[k], core_id + k, at(c=peer))

    a_id, b_id = ids(3 * CH), ids(3 * CH)
    rows = 128 // CH

    def a_copy(slot, piece):
        own = pl.ds(piece * rows, rows)
        src = fa.at[own] if slot == 2 else zs.at[slot, own]
        return remote(src, ra.at[slot, own], a_id + slot * CH + piece, at(p=p1))

    def b_copy(slot, piece):
        own = pl.ds(piece * rows, rows)
        src = fb.at[own] if slot == 2 else zs.at[2 * slot, pl.ds(128 + piece * rows, rows)]
        return remote(src, rb.at[slot, own], b_id + slot * CH + piece, at(p=p3))

    for load in loads[2:]:
        load.wait()

    def teacher_step(k, carry):
        q = jnp.where(k == 0, p2, jnp.where(k == 1, p1, jnp.where(k == 2, p3, p)))
        tokens = pl.ds(pl.multiple_of(q * 256, 256), 256)
        hidden = hid[tokens, :]
        for low, high in ((0, STEP), (STEP, DT)):
            part[:, low:high] = (
                jnp.dot(hidden, w[:, low:high], preferred_element_type=F32) * ls_ref[:, low:high]
            )
        window = pl.ds(pl.multiple_of(384 * t, 128), WIDE)
        part[:, window] += jnp.dot(res[tokens, :], sel, preferred_element_type=F32)
        cs[k] = part[:, pl.ds(pl.multiple_of(STEP * peer, 128), HALF)].astype(BF16)
        core_copy(k).start()
        core_copy(k).wait_recv()
        own = part[:, pl.ds(pl.multiple_of(STEP * c, 128), HALF)]
        zs[k] = (own + wide(cr[k])).astype(BF16)

        @pl.when(k == 0)
        def _():
            for piece in range(CH):
                a_copy(0, piece).start()
                b_copy(0, piece).start()

        @pl.when(k == 1)
        def _():
            for piece in range(CH):
                a_copy(1, piece).start()
            head_first()

        @pl.when(k == 3)
        def _():
            head_second()

        return carry

    lax.fori_loop(0, 4, teacher_step, 0)

    def normalize(values):
        centered = values - jnp.mean(values, axis=1, keepdims=True)
        inverse = lax.rsqrt(jnp.mean(centered * centered, axis=1, keepdims=True) + epsilon)
        return centered * inverse, inverse

    x_copy().wait_recv()
    for h in range(2):
        normed, _ = normalize(wide(xs[h]))
        out = (normed * gain_ref[...]).astype(BF16)
        nb[h * 128 : (h + 1) * 128, :] = out
        nt[:, h * 128 : (h + 1) * 128] = jnp.transpose(wide(out)).astype(BF16)

    for piece in range(CH):
        low = piece * rows
        a_copy(0, piece).wait_recv()
        fb[low : low + rows, :] = (
            wide(zs[2, low : low + rows, :]) + wide(ra[0, low : low + rows, :])
        ).astype(BF16)
        b_copy(2, piece).start()
        b_copy(1, piece).start()
        b_copy(0, piece).wait_recv()
        fa[low : low + rows, :] = (
            wide(zs[1, 128 + low : 128 + low + rows, :]) + wide(rb[0, low : low + rows, :])
        ).astype(BF16)
        a_copy(2, piece).start()

    for o in range(1, 4):
        for m in range(2):
            h2_copy(m, o).wait_recv()
    head = hd[...].reshape(1024, HALF)
    pr[...] = jnp.dot(nb[...], head, preferred_element_type=F32)

    lane = lax.broadcasted_iota(jnp.int32, (1, HALF), 1)
    mine = (lane >= 128 * c).astype(F32)
    small = lax.broadcasted_iota(jnp.int32, (128, 128), 1)

    stat_id = ids(2)

    def stat_copy(h):
        return remote(st.at[h], sr.at[h], stat_id + h, at(c=peer))

    def finish(h):
        block = slice(h * 128, (h + 1) * 128)
        one, two = (ra, rb) if h == 0 else (rb, ra)
        for piece in range(CH):
            (a_copy if h == 0 else b_copy)(1, piece).wait_recv()
            (b_copy if h == 0 else a_copy)(2, piece).wait_recv()
        total = wide(zs[3, block, :]) + wide(one[1]) + wide(two[2])
        target = wide(total.astype(BF16))
        predicted = pr[block, :]
        masked = predicted * mine
        inner = jnp.sum(masked * target, axis=1, keepdims=True)
        square = jnp.sum(masked * predicted, axis=1, keepdims=True)
        aim = jnp.sum(target * target * mine, axis=1, keepdims=True)
        st[h] = jnp.where(small == 0, inner, jnp.where(small == 1, square, aim))
        stat_copy(h).start()
        stat_copy(h).wait_recv()
        both = st[h] + sr[h]
        inner, square, aim = both[:, 0:1], both[:, 1:2], both[:, 2:3]
        scaling = lax.rsqrt((square + epsilon) * (aim + epsilon))
        cosine = inner * scaling
        pg[block, :] = (
            (cosine / (square + epsilon)) * predicted - scaling * target
        ).astype(BF16)

        @pl.when(c == h)
        def _():
            loss = jnp.broadcast_to(1.0 - cosine, (128, 128))
            loss_ref[...] = jnp.transpose(loss)[0:1, :]

    def back(h):
        bp[h] = lax.dot_general(
            pg[h * 128 : (h + 1) * 128, :] * mine.astype(BF16),
            hd[...].reshape(1024, HALF),
            (((1,), (1,)), ((), ())),
            preferred_element_type=F32,
        )

    finish(0)
    back(0)
    finish(1)

    def grad_step(k, carry):
        piece = jnp.dot(
            nt[pl.ds(pl.multiple_of(k * 128, 128), 128), :], pg[...], preferred_element_type=F32
        ).astype(BF16)
        for j in range(4):
            block = piece[j * 32 : (j + 1) * 32, :]

            @pl.when(k < 4)
            def _():
                gs[0, k, j] = block

            @pl.when(k >= 4)
            def _():
                gs[1, j, k - 4] = block

        return carry

    lax.fori_loop(0, 8, grad_step, 0)

    g_id = ids(12)

    def g_copy(m, way, slot):
        a = x if m == 0 else y
        near, far, last = a + 1 - 2 * (a % 2), (a + 2) % 4, 3 - a
        to = near if way == 0 else last
        device = at(x=to) if m == 0 else at(y=to)
        if slot == 2:
            src = f1.at[m, way]
        else:
            src = gs.at[m, far if slot == 0 else to, pl.ds(2 * way, 2)]
        return remote(src, r1.at[m, way, slot], g_id + m * 6 + way * 3 + slot, device)

    for slot in range(2):
        for m in range(2):
            for way in range(2):
                g_copy(m, way, slot).start()

    back(1)
    back_id = ids(1)

    def back_copy():
        return remote(bp.at[peer], br, back_id, at(c=peer))

    back_copy().start()

    for m in range(2):
        a = x if m == 0 else y
        near, last = a + 1 - 2 * (a % 2), 3 - a
        for way in range(2):
            g_copy(m, way, 0).wait_recv()
        f1[m, 1] = (wide(gs[m, last, 0:2]) + wide(r1[m, 0, 0])).astype(BF16)
        g_copy(m, 1, 2).start()
        f1[m, 0] = (wide(gs[m, near, 2:4]) + wide(r1[m, 1, 0])).astype(BF16)
        g_copy(m, 0, 2).start()

    back_copy().wait_recv()
    normed, inverse = normalize(wide(xs[c]))
    normed_grad = (bp[c] + br[...]) * gain_ref[...]
    igrad_ref[...] = (
        inverse
        * (
            normed_grad
            - jnp.mean(normed_grad, axis=1, keepdims=True)
            - normed * jnp.mean(normed_grad * normed, axis=1, keepdims=True)
        )
    ).astype(BF16)

    g2_id = ids(6)

    def g2_copy(m, o):
        b = y if m == 0 else x
        to = (b + o) % 4
        device = at(y=to) if m == 0 else at(x=to)
        return remote(s1.at[m, to], r2.at[m, o - 1], g2_id + 3 * m + o - 1, device)

    for m in range(2):
        a = x if m == 0 else y
        for way in range(2):
            g_copy(m, way, 1).wait_recv()
        for way in range(2):
            g_copy(m, way, 2).wait_recv()
        for way in range(2):
            s1[m, 2 * way : 2 * way + 2] = (
                wide(gs[m, a, 2 * way : 2 * way + 2])
                + wide(r1[m, way, 1])
                + wide(r1[m, 1 - way, 2])
            ).astype(BF16)
        for o in (1, 3, 2):
            g2_copy(m, o).start()
    for m in range(2):
        b = y if m == 0 else x
        total = wide(s1[m, b])
        for o in range(1, 4):
            g2_copy(m, o).wait_recv()
            total = total + wide(r2[m, o - 1])
        s2[m] = total.astype(BF16)

    g3_id = ids(8)

    def window_of(to):
        return pl.ds(pl.multiple_of(768 * ((to // 2) % 2), 128), OUTW)

    def g3_copy(o):
        to = (zz + o) % 8
        src = s2.at[to % 2, :, window_of(to)]
        return remote(src, rz.at[o], g3_id + o, at(zl=to % 2, p=to // 2))

    for o in (1, 7, 2, 6, 3, 5, 4):

        @pl.when(((zz + o) % 8) // 4 == c)
        def _():
            g3_copy(o).start()

    end_id = ids(1)

    def end_copy():
        return remote(hgs, hgs, end_id, at(c=peer))

    @pl.when(p // 2 == c)
    def _():
        total = wide(s2[zl, :, window_of(zz)])
        for o in range(1, 8):
            g3_copy(o).wait_recv()
            total = total + wide(rz[o])
        hgs[...] = total.astype(BF16)
        end_copy().start()
        end_copy().wait_send()

    @pl.when(p // 2 != c)
    def _():
        end_copy().wait_recv()

    hgrad_ref[...] = hgs[...]

    x_copy().wait_send()
    for o in range(1, 4):
        hz_copy(o).wait_send()
        for m in range(2):
            h1_copy(m, o).wait_send()
            h2_copy(m, o).wait_send()
            g2_copy(m, o).wait_send()
    for o in range(4):
        hc_copy(o).wait_send()
        core_copy(o).wait_send()
    for slot in range(3):
        for piece in range(CH):
            a_copy(slot, piece).wait_send()
            b_copy(slot, piece).wait_send()
        for m in range(2):
            for way in range(2):
                g_copy(m, way, slot).wait_send()
    for h in range(2):
        stat_copy(h).wait_send()
    back_copy().wait_send()
    for o in range(1, 8):

        @pl.when(((zz + o) % 8) // 4 == c)
        def _():
            g3_copy(o).wait_send()


def shards(
    teacher_hidden, down_weight, teacher_resid, layer_scale, student_x, norm_gain, head_weight
):
    hbm = pl.BlockSpec(memory_space=pl.ANY)
    vmem = pl.BlockSpec(memory_space=pltpu.VMEM)
    scratch = [
        ((1024, 800), BF16),
        ((800, DT), BF16),
        ((1024, 400), BF16),
        ((64, 400), BF16),
        ((256, DT), F32),
        ((4, 256, HALF), BF16),
        ((4, 256, HALF), BF16),
        ((4, 256, HALF), BF16),
        ((3, 128, HALF), BF16),
        ((3, 128, HALF), BF16),
        ((128, HALF), BF16),
        ((128, HALF), BF16),
        ((10, 64, WIDE), BF16),
        ((4, 4, 64, HALF), BF16),
        ((2, 128, 1024), BF16),
        ((256, 1024), BF16),
        ((1024, 256), BF16),
        ((256, HALF), F32),
        ((256, HALF), BF16),
        ((2, 128, 128), F32),
        ((2, 128, 128), F32),
        ((2, 128, 1024), F32),
        ((128, 1024), F32),
        ((2, 4, 4, 32, HALF), BF16),
        ((2, 2, 3, 2, 32, HALF), BF16),
        ((2, 2, 2, 32, HALF), BF16),
        ((2, 4, 32, HALF), BF16),
        ((2, 3, 32, HALF), BF16),
        ((2, 32, HALF), BF16),
        ((8, 32, OUTW), BF16),
        ((32, OUTW), BF16),
    ]
    copies = 1 + 3 + 4 + 6 + 6 + 4 + 6 * CH + 2 + 12 + 1 + 6 + 8 + 1
    loss, input_grad, head_grad = pl.pallas_call(
        kernel,
        name="distill",
        out_shape=(
            jax.ShapeDtypeStruct((1, 128), F32),
            jax.ShapeDtypeStruct((128, 1024), BF16),
            jax.ShapeDtypeStruct((32, OUTW), BF16),
        ),
        in_specs=[hbm, hbm, hbm, vmem, hbm, vmem, hbm],
        out_specs=(vmem, vmem, vmem),
        scratch_shapes=[pltpu.VMEM(shape, kind) for shape, kind in scratch]
        + [
            pltpu.SemaphoreType.DMA((5,)),
            pltpu.SemaphoreType.DMA((copies,)),
            pltpu.SemaphoreType.DMA((copies,)),
        ],
        compiler_params=pltpu.CompilerParams(
            collective_id=0, has_side_effects=True, vmem_limit_bytes=60 * 2**20
        ),
        cost_estimate=pl.CostEstimate(
            flops=8_000_000_000, bytes_accessed=10_000_000, transcendentals=1000
        ),
    )(
        teacher_hidden,
        down_weight,
        teacher_resid,
        layer_scale.reshape(1, DT),
        student_x,
        norm_gain.reshape(1, -1),
        head_weight,
    )
    t = lax.axis_index("tensor")
    first = 32 * (t // 2) + 400 * (t % 2)
    head_grad = lax.dynamic_slice_in_dim(head_grad, first, 400, axis=1)
    return (loss.reshape(-1), input_grad, head_grad)


def solution(mesh):
    placed = (
        P("dp", "tensor"),
        P("tensor", None),
        P("dp", "tensor"),
        P(),
        P(("dp", "tensor"), None),
        P(),
        P(None, "tensor"),
    )
    return jax.shard_map(
        shards,
        mesh=mesh,
        in_specs=placed,
        out_specs=(P(("dp", "tensor")), P(("dp", "tensor"), None), P("dp", "tensor")),
        check_vma=False,
    )
```

```python
import functools

import jax
import jax.numpy as jnp
from jax import lax
from jax.experimental import pallas as pl
from jax.experimental.pallas import tpu as pltpu
from jax.sharding import PartitionSpec as P

MESH = pl.DeviceIdType.MESH
F32 = jnp.float32
BF16 = jnp.bfloat16
epsilon = 1e-06

DT = 3200
HALF = 1664
STEP = 1536
WIDE = 512
OUTW = 896
CH = 4


def wide(value):
    return value.astype(F32)


def across(left, right):
    return lax.dot_general(left, right, (((0,), (0,)), ((), ())), preferred_element_type=F32)


def kernel(
    hid_hbm, w_hbm, res_hbm, ls_ref, x_hbm, gain_ref, head_hbm,
    loss_ref, igrad_ref, hgrad_ref,
    hid, w, res, hrow, htwo, lsrow, part, cs, cr, zs, ra, rb, fa, fb, hw, hd, xs, nb, nt, pr, pg,
    squares, tg, losses, st, sr, bp, br, gs, r1, f1, s1, r2, s2, rz, hgs,
    lsem, ssem, rsem,
):
    d = lax.axis_index("dp")
    t = lax.axis_index("tensor")
    zl, x, y = d // 16, (d // 4) % 4, d % 4
    p, c = t // 2, t % 2
    p1, p2, p3 = p + 1 - 2 * (p % 2), (p + 2) % 4, 3 - p
    peer = 1 - c

    def at(zl=zl, x=x, y=y, p=p, c=c):
        return {"dp": zl * 16 + x * 4 + y, "tensor": p * 2 + c}

    counts = [0]

    def ids(n):
        first = counts[0]
        counts[0] += n
        return first

    def remote(src, dst, j, device):
        return pltpu.make_async_remote_copy(
            src_ref=src, dst_ref=dst, send_sem=ssem.at[j], recv_sem=rsem.at[j],
            device_id=device, device_id_type=MESH,
        )

    row_block = x * 4 + y
    loads = [
        pltpu.make_async_copy(
            head_hbm.at[:, pl.ds(pl.multiple_of(row_block // 2 * 128, 128), 128)], hrow, lsem.at[0]
        ),
        pltpu.make_async_copy(x_hbm, xs.at[c], lsem.at[1]),
        pltpu.make_async_copy(w_hbm, w, lsem.at[2]),
        pltpu.make_async_copy(hid_hbm, hid, lsem.at[3]),
        pltpu.make_async_copy(res_hbm, res, lsem.at[4]),
    ]
    for load in loads:
        load.start()

    barrier = pltpu.get_barrier_semaphore()
    zz = p * 2 + zl
    greeted = [at(c=peer)]
    for o in range(1, 8):
        other = (zz + o) % 8
        greeted.append(at(zl=other % 2, p=other // 2))
    for o in range(1, 4):
        greeted.append(at(x=(x + o) % 4))
        greeted.append(at(y=(y + o) % 4))
    for device in greeted:
        pl.semaphore_signal(barrier, inc=1, device_id=device, device_id_type=MESH)

    spot = lax.broadcasted_iota(jnp.int32, (400, WIDE), 1)
    sel = (spot == lax.broadcasted_iota(jnp.int32, (400, WIDE), 0) + 16 * t).astype(BF16)
    hw[0] = jnp.zeros((64, WIDE), BF16)
    hw[9] = jnp.zeros((64, WIDE), BF16)
    loads[0].wait()
    htwo[...] = across(hrow[...], sel)
    hw[1 + t] = htwo[pl.ds(pl.multiple_of(row_block % 2 * 64, 64), 64), :].astype(BF16)
    for j in range(25):
        lsrow[:, j * 128 : (j + 1) * 128] = ls_ref[j : j + 1, :]

    pl.semaphore_wait(barrier, len(greeted))

    x_id = ids(1)

    def x_copy():
        return remote(xs.at[c], xs.at[c], x_id, at(c=peer))

    loads[1].wait()
    x_copy().start()

    hz_id = ids(3)

    def hz_copy(o):
        return remote(hw.at[1 + t], hw.at[1 + t], hz_id + o - 1, at(p=(p + o) % 4))

    for o in (1, 3, 2):
        hz_copy(o).start()

    hc_id = ids(4)

    def hc_copy(o):
        slot = 1 + 2 * ((p + 4 - o) % 4) + c
        return remote(hw.at[slot], hw.at[slot], hc_id + o, at(c=peer))

    h1_id = ids(6)

    def h1_copy(m, o):
        block = hd.at[x, y, :, pl.ds(896 * m, 896 - 128 * m)]
        device = at(x=(x + o) % 4) if m == 0 else at(y=(y + o) % 4)
        return remote(block, block, h1_id + 3 * m + o - 1, device)

    h2_id = ids(6)

    def h2_copy(m, o):
        if m == 0:
            block, device = hd.at[:, y, :, pl.ds(0, 896)], at(y=(y + o) % 4)
        else:
            block, device = hd.at[x, :, :, pl.ds(896, 768)], at(x=(x + o) % 4)
        return remote(block, block, h2_id + 3 * m + o - 1, device)

    def head_first():
        for o in range(4):
            if o:
                hz_copy(o).wait_recv()
            hc_copy(o).start()
        for o in range(4):
            hc_copy(o).wait_recv()
        for j in range(13):
            tile = hw[1 + 4 * c + j // 3, :, (j % 3) * 128 : (j % 3) * 128 + 128]
            if j % 3 == 0:
                tile = tile + hw[4 * c + j // 3, :, 384:512]
            hd[x, y, :, j * 128 : (j + 1) * 128] = tile
        for o in (1, 3, 2):
            for m in range(2):
                h1_copy(m, o).start()

    def head_second():
        for o in range(1, 4):
            for m in range(2):
                h1_copy(m, o).wait_recv()
        for o in (1, 3, 2):
            for m in range(2):
                h2_copy(m, o).start()

    core_id = ids(4)

    def core_copy(k):
        return remote(cs.at[k], cr.at[k], core_id + k, at(c=peer))

    a_id, b_id = ids(3 * CH), ids(3 * CH)
    rows = 128 // CH

    def a_copy(slot, piece):
        own = pl.ds(piece * rows, rows)
        src = fa.at[own] if slot == 2 else zs.at[slot, own]
        return remote(src, ra.at[slot, own], a_id + slot * CH + piece, at(p=p1))

    def b_copy(slot, piece):
        own = pl.ds(piece * rows, rows)
        src = fb.at[own] if slot == 2 else zs.at[2 * slot, pl.ds(128 + piece * rows, rows)]
        return remote(src, rb.at[slot, own], b_id + slot * CH + piece, at(p=p3))

    for load in loads[2:]:
        load.wait()

    def teacher_step(k, carry):
        q = jnp.where(k == 0, p2, jnp.where(k == 1, p1, jnp.where(k == 2, p3, p)))
        tokens = pl.ds(pl.multiple_of(q * 256, 256), 256)
        hidden = jnp.transpose(hid[:, tokens])
        for low, high in ((0, STEP), (STEP, DT)):
            part[:, low:high] = (
                jnp.dot(hidden, w[:, low:high], preferred_element_type=F32) * lsrow[:, low:high]
            )
        window = pl.ds(pl.multiple_of(384 * t, 128), WIDE)
        part[:, window] += across(res[:, tokens], sel)
        cs[k] = part[:, pl.ds(pl.multiple_of(STEP * peer, 128), HALF)].astype(BF16)
        core_copy(k).start()
        core_copy(k).wait_recv()
        own = part[:, pl.ds(pl.multiple_of(STEP * c, 128), HALF)]
        zs[k] = (own + wide(cr[k])).astype(BF16)

        @pl.when(k == 0)
        def _():
            for piece in range(CH):
                a_copy(0, piece).start()
                b_copy(0, piece).start()

        @pl.when(k == 1)
        def _():
            for piece in range(CH):
                a_copy(1, piece).start()
            head_first()

        @pl.when(k == 3)
        def _():
            head_second()

        return carry

    lax.fori_loop(0, 4, teacher_step, 0)

    def normalize(values):
        centered = values - jnp.mean(values, axis=1, keepdims=True)
        inverse = lax.rsqrt(jnp.mean(centered * centered, axis=1, keepdims=True) + epsilon)
        return centered * inverse, inverse

    x_copy().wait_recv()
    for h in range(2):
        normed, _ = normalize(wide(xs[h]))
        out = (normed * gain_ref[...]).astype(BF16)
        nb[h * 128 : (h + 1) * 128, :] = out
        turned = jnp.transpose(wide(out)).astype(BF16)
        nt[:, :, :, :, h * 128 : (h + 1) * 128] = turned.reshape(2, 4, 4, 32, 128)

    for piece in range(CH):
        low = piece * rows
        a_copy(0, piece).wait_recv()
        fb[low : low + rows, :] = (
            wide(zs[2, low : low + rows, :]) + wide(ra[0, low : low + rows, :])
        ).astype(BF16)
        b_copy(2, piece).start()
        b_copy(1, piece).start()
        b_copy(0, piece).wait_recv()
        fa[low : low + rows, :] = (
            wide(zs[1, 128 + low : 128 + low + rows, :]) + wide(rb[0, low : low + rows, :])
        ).astype(BF16)
        a_copy(2, piece).start()

    for o in range(1, 4):
        for m in range(2):
            h2_copy(m, o).wait_recv()
    head = hd[...].reshape(1024, HALF)
    pr[...] = jnp.dot(nb[...], head, preferred_element_type=F32)

    lane = lax.broadcasted_iota(jnp.int32, (1, HALF), 1)
    mine = (lane >= 128 * c).astype(F32)
    small = lax.broadcasted_iota(jnp.int32, (rows, 128), 1)

    stat_id = ids(2 * CH)

    def stat_copy(h, piece):
        own = pl.ds(piece * rows, rows)
        return remote(st.at[h, own], sr.at[h, own], stat_id + h * CH + piece, at(c=peer))

    square_all = jnp.sum(pr[...] * pr[...] * mine, axis=1, keepdims=True)
    squares[...] = jnp.broadcast_to(square_all, (256, 128))

    def finish(h):
        one, two = (ra, rb) if h == 0 else (rb, ra)
        for piece in range(CH):
            (a_copy if h == 0 else b_copy)(1, piece).wait_recv()
            (b_copy if h == 0 else a_copy)(2, piece).wait_recv()
            own = slice(piece * rows, (piece + 1) * rows)
            block = slice(h * 128 + piece * rows, h * 128 + (piece + 1) * rows)
            total = wide(zs[3, block, :]) + wide(one[1, own, :]) + wide(two[2, own, :])
            target = total.astype(BF16)
            tg[block, :] = target
            target = wide(target)
            masked = target * mine
            inner = jnp.sum(masked * pr[block, :], axis=1, keepdims=True)
            aim = jnp.sum(masked * target, axis=1, keepdims=True)
            st[h, own, :] = jnp.where(
                small == 0, inner, jnp.where(small == 1, squares[block, :], aim)
            )
            stat_copy(h, piece).start()
        for piece in range(CH):
            own = slice(piece * rows, (piece + 1) * rows)
            block = slice(h * 128 + piece * rows, h * 128 + (piece + 1) * rows)
            stat_copy(h, piece).wait_recv()
            both = st[h, own, :] + sr[h, own, :]
            inner, square, aim = both[:, 0:1], both[:, 1:2], both[:, 2:3]
            scaling = lax.rsqrt((square + epsilon) * (aim + epsilon))
            cosine = inner * scaling
            pg[block, :] = (
                (cosine / (square + epsilon)) * pr[block, :] - scaling * wide(tg[block, :])
            ).astype(BF16)
            losses[own, :] = jnp.broadcast_to(1.0 - cosine, (rows, 128))

        @pl.when(c == h)
        def _():
            loss_ref[...] = jnp.transpose(losses[...])[0:1, :]

    def back(h):
        bp[h] = lax.dot_general(
            pg[h * 128 : (h + 1) * 128, :] * mine.astype(BF16),
            hd[...].reshape(1024, HALF),
            (((1,), (1,)), ((), ())),
            preferred_element_type=F32,
        )

    finish(0)
    back(0)
    finish(1)

    parts = (pl.ds(0, OUTW), pl.ds(OUTW, HALF - OUTW))
    g_id = ids(24)
    axes = []
    for m in range(2):
        a = x if m == 0 else y
        axes.append((a, a + 1 - 2 * (a % 2), (a + 2) % 4, 3 - a))

    def g_copy(n, m, way, slot):
        a, near, far, last = axes[m]
        to = near if way == 0 else last
        device = at(x=to) if m == 0 else at(y=to)
        if slot == 2:
            src = f1.at[m, way, :, :, parts[n]]
        else:
            src = gs.at[m, far if slot == 0 else to, pl.ds(2 * way, 2), :, parts[n]]
        dst = r1.at[m, way, slot, :, :, parts[n]]
        return remote(src, dst, g_id + n * 12 + m * 6 + way * 3 + slot, device)

    def gradient(n, turn):
        ax, ay = axes[0][turn], axes[1][turn]
        left = jnp.concatenate(
            [nt[0, ax].reshape(128, 256), nt[1, :, ay].reshape(128, 256)], axis=0
        )
        both = jnp.dot(left, pg[:, parts[n]], preferred_element_type=F32).astype(BF16)
        gs[0, ax, :, :, parts[n]] = both[0:128].reshape(4, 32, -1)
        gs[1, ay, :, :, parts[n]] = both[128:256].reshape(4, 32, -1)

    def first_sends(n, slot):
        for m in range(2):
            for way in range(2):
                g_copy(n, m, way, slot).start()

    def forward(n):
        for m in range(2):
            a, near, far, last = axes[m]
            for way in range(2):
                g_copy(n, m, 1 - way, 0).wait_recv()
                target, inner = (near, slice(2, 4)) if way == 0 else (last, slice(0, 2))
                f1[m, way, :, :, parts[n]] = (
                    wide(gs[m, target, inner, :, parts[n]])
                    + wide(r1[m, 1 - way, 0, :, :, parts[n]])
                ).astype(BF16)
                g_copy(n, m, way, 2).start()

    g2_id = ids(12)

    def g2_copy(n, m, o):
        b = y if m == 0 else x
        to = (b + o) % 4
        device = at(y=to) if m == 0 else at(x=to)
        return remote(
            s1.at[m, to, :, parts[n]], r2.at[m, o - 1, :, parts[n]],
            g2_id + 6 * n + 3 * m + o - 1, device,
        )

    def second_sends(n):
        for m in range(2):
            a = axes[m][0]
            for slot in (1, 2):
                for way in range(2):
                    g_copy(n, m, way, slot).wait_recv()
            for way in range(2):
                inner = slice(2 * way, 2 * way + 2)
                s1[m, inner, :, parts[n]] = (
                    wide(gs[m, a, inner, :, parts[n]])
                    + wide(r1[m, way, 1, :, :, parts[n]])
                    + wide(r1[m, 1 - way, 2, :, :, parts[n]])
                ).astype(BF16)
            for o in (1, 3, 2):
                g2_copy(n, m, o).start()

    def second_sums(n):
        for m in range(2):
            total = wide(s1[m, axes[1 - m][0], :, parts[n]])
            for o in range(1, 4):
                g2_copy(n, m, o).wait_recv()
                total = total + wide(r2[m, o - 1, :, parts[n]])
            s2[m, :, parts[n]] = total.astype(BF16)

    g3_id = ids(8)

    def window_of(to):
        return pl.ds(pl.multiple_of(768 * ((to // 2) % 2), 128), OUTW)

    def g3_copy(o):
        to = (zz + o) % 8
        src = s2.at[to % 2, :, window_of(to)]
        return remote(src, rz.at[o], g3_id + o, at(zl=to % 2, p=to // 2))

    def third_sends(n):
        for o in (1, 7, 2, 6, 3, 5, 4):
            chip = ((zz + o) % 8) // 2

            @pl.when((chip // 2 == c) & (chip % 2 == n))
            def _():
                g3_copy(o).start()

    gradient(0, 2)
    first_sends(0, 0)
    gradient(0, 1)
    gradient(0, 3)
    first_sends(0, 1)
    gradient(0, 0)
    for turn in range(4):
        gradient(1, turn)
    forward(0)
    first_sends(1, 0)
    first_sends(1, 1)

    back(1)
    back_id = ids(1)

    def back_copy():
        return remote(bp.at[peer], br, back_id, at(c=peer))

    back_copy().start()
    second_sends(0)
    forward(1)

    back_copy().wait_recv()
    normed, inverse = normalize(wide(xs[c]))
    normed_grad = (bp[c] + br[...]) * gain_ref[...]
    igrad_ref[...] = (
        inverse
        * (
            normed_grad
            - jnp.mean(normed_grad, axis=1, keepdims=True)
            - normed * jnp.mean(normed_grad * normed, axis=1, keepdims=True)
        )
    ).astype(BF16)

    second_sums(0)
    third_sends(0)
    second_sends(1)
    second_sums(1)
    third_sends(1)

    end_id = ids(1)

    def end_copy():
        return remote(hgs, hgs, end_id, at(c=peer))

    @pl.when(p // 2 == c)
    def _():
        total = wide(s2[zl, :, window_of(zz)])
        for o in range(1, 8):
            g3_copy(o).wait_recv()
            total = total + wide(rz[o])
        hgs[...] = total.astype(BF16)
        end_copy().start()
        end_copy().wait_send()

    @pl.when(p // 2 != c)
    def _():
        end_copy().wait_recv()

    hgrad_ref[...] = hgs[...]

    x_copy().wait_send()
    for o in range(1, 4):
        hz_copy(o).wait_send()
        for m in range(2):
            h1_copy(m, o).wait_send()
            h2_copy(m, o).wait_send()
            for n in range(2):
                g2_copy(n, m, o).wait_send()
    for o in range(4):
        hc_copy(o).wait_send()
        core_copy(o).wait_send()
    for slot in range(3):
        for piece in range(CH):
            a_copy(slot, piece).wait_send()
            b_copy(slot, piece).wait_send()
        for m in range(2):
            for way in range(2):
                for n in range(2):
                    g_copy(n, m, way, slot).wait_send()
    for h in range(2):
        for piece in range(CH):
            stat_copy(h, piece).wait_send()
    back_copy().wait_send()
    for o in range(1, 8):

        @pl.when(((zz + o) % 8) // 4 == c)
        def _():
            g3_copy(o).wait_send()


def place(loss_ref, igrad_ref, hgrad_ref, loss_out, igrad_out, hgrad_out):
    loss_out[...] = loss_ref[...]
    igrad_out[...] = igrad_ref[...]
    t = lax.axis_index("tensor")
    first = 32 * (t // 2) + 400 * (t % 2)
    row = lax.broadcasted_iota(jnp.int32, (OUTW, 400), 0)
    pick = (row == lax.broadcasted_iota(jnp.int32, (OUTW, 400), 1) + first).astype(BF16)
    hgrad_out[...] = jnp.dot(hgrad_ref[...], pick, preferred_element_type=F32).astype(BF16)


def shards(
    teacher_hidden, down_weight, teacher_resid, layer_scale, student_x, norm_gain, head_weight
):
    hbm = pl.BlockSpec(memory_space=pl.ANY)
    vmem = pl.BlockSpec(memory_space=pltpu.VMEM)
    scratch = [
        ((800, 1024), BF16),
        ((800, DT), BF16),
        ((400, 1024), BF16),
        ((400, 128), BF16),
        ((128, WIDE), F32),
        ((1, DT), F32),
        ((256, DT), F32),
        ((4, 256, HALF), BF16),
        ((4, 256, HALF), BF16),
        ((4, 256, HALF), BF16),
        ((3, 128, HALF), BF16),
        ((3, 128, HALF), BF16),
        ((128, HALF), BF16),
        ((128, HALF), BF16),
        ((10, 64, WIDE), BF16),
        ((4, 4, 64, HALF), BF16),
        ((2, 128, 1024), BF16),
        ((256, 1024), BF16),
        ((2, 4, 4, 32, 256), BF16),
        ((256, HALF), F32),
        ((256, HALF), BF16),
        ((256, 128), F32),
        ((256, HALF), BF16),
        ((128, 128), F32),
        ((2, 128, 128), F32),
        ((2, 128, 128), F32),
        ((2, 128, 1024), F32),
        ((128, 1024), F32),
        ((2, 4, 4, 32, HALF), BF16),
        ((2, 2, 3, 2, 32, HALF), BF16),
        ((2, 2, 2, 32, HALF), BF16),
        ((2, 4, 32, HALF), BF16),
        ((2, 3, 32, HALF), BF16),
        ((2, 32, HALF), BF16),
        ((8, 32, OUTW), BF16),
        ((32, OUTW), BF16),
    ]
    copies = 1 + 3 + 4 + 6 + 6 + 4 + 6 * CH + 2 * CH + 24 + 12 + 8 + 1 + 1
    loss, input_grad, head_grad = pl.pallas_call(
        kernel,
        name="distill",
        out_shape=(
            jax.ShapeDtypeStruct((1, 128), F32),
            jax.ShapeDtypeStruct((128, 1024), BF16),
            jax.ShapeDtypeStruct((32, OUTW), BF16),
        ),
        in_specs=[hbm, hbm, hbm, vmem, hbm, vmem, hbm],
        out_specs=(vmem, vmem, vmem),
        scratch_shapes=[pltpu.VMEM(shape, kind) for shape, kind in scratch]
        + [
            pltpu.SemaphoreType.DMA((5,)),
            pltpu.SemaphoreType.DMA((copies,)),
            pltpu.SemaphoreType.DMA((copies,)),
        ],
        compiler_params=pltpu.CompilerParams(
            collective_id=0, has_side_effects=True, vmem_limit_bytes=60 * 2**20
        ),
        cost_estimate=pl.CostEstimate(
            flops=8_000_000_000, bytes_accessed=10_000_000, transcendentals=1000
        ),
    )(
        teacher_hidden.T,
        down_weight,
        teacher_resid.T,
        layer_scale.reshape(25, 128),
        student_x,
        norm_gain.reshape(1, -1),
        head_weight.T,
    )
    loss, input_grad, head_grad = pl.pallas_call(
        place,
        name="place",
        out_shape=(
            jax.ShapeDtypeStruct((1, 128), F32),
            jax.ShapeDtypeStruct((128, 1024), BF16),
            jax.ShapeDtypeStruct((32, 400), BF16),
        ),
        in_specs=[vmem, vmem, vmem],
        out_specs=(vmem, vmem, vmem),
    )(loss, input_grad, head_grad)
    return (loss.reshape(-1), input_grad, head_grad)


def solution(mesh):
    placed = (
        P("dp", "tensor"),
        P("tensor", None),
        P("dp", "tensor"),
        P(),
        P(("dp", "tensor"), None),
        P(),
        P(None, "tensor"),
    )
    return jax.shard_map(
        shards,
        mesh=mesh,
        in_specs=placed,
        out_specs=(P(("dp", "tensor")), P(("dp", "tensor"), None), P("dp", "tensor")),
        check_vma=False,
    )
```

```python
import functools

import jax
import jax.numpy as jnp
from jax import lax
from jax.experimental import pallas as pl
from jax.experimental.pallas import tpu as pltpu
from jax.sharding import PartitionSpec as P

MESH = pl.DeviceIdType.MESH
F32 = jnp.float32
BF16 = jnp.bfloat16
epsilon = 1e-06

DT = 3200
HALF = 1664
STEP = 1536
WIDE = 512
CH = 2


def wide(value):
    return value.astype(F32)


def across(left, right):
    return lax.dot_general(left, right, (((0,), (0,)), ((), ())), preferred_element_type=F32)


def kernel(
    hid_hbm, w_hbm, res_hbm, ls_ref, x_hbm, gain_ref, head_hbm,
    loss_ref, igrad_ref, hgrad_ref,
    hid, hq, rq, w, res, hrow, htwo, lsrow, part, cs, cr, zs, ra, rb, fa, fb, hw, hd, xs, nb, nt, pr, pg,
    squares, tg, losses, st, sr, bp, br, gs0, gs1, r10, r11, f10, f11, s10, s11, r20, r21, s2, rz,
    lsem, ssem, rsem,
):
    d = lax.axis_index("dp")
    t = lax.axis_index("tensor")
    zl, x, y = d // 16, (d // 4) % 4, d % 4
    p, c = t // 2, t % 2
    p1, p2, p3 = p + 1 - 2 * (p % 2), (p + 2) % 4, 3 - p
    peer = 1 - c

    def at(zl=zl, x=x, y=y, p=p, c=c):
        return {"dp": zl * 16 + x * 4 + y, "tensor": p * 2 + c}

    counts = [0]

    def ids(n):
        first = counts[0]
        counts[0] += n
        return first

    def remote(src, dst, j, device):
        return pltpu.make_async_remote_copy(
            src_ref=src, dst_ref=dst, send_sem=ssem.at[j], recv_sem=rsem.at[j],
            device_id=device, device_id_type=MESH,
        )

    row_block = x * 4 + y
    cuts = ((0, 208), (208, 208), (416, 192), (608, 192))
    loads = [
        pltpu.make_async_copy(hid_hbm, hid, lsem.at[0]),
        pltpu.make_async_copy(res_hbm, res, lsem.at[1]),
        pltpu.make_async_copy(
            head_hbm.at[:, pl.ds(pl.multiple_of(row_block // 2 * 128, 128), 128)], hrow, lsem.at[2]
        ),
        pltpu.make_async_copy(x_hbm, xs.at[c], lsem.at[3]),
    ] + [
        pltpu.make_async_copy(w_hbm.at[pl.ds(low, n)], w.at[pl.ds(low, n)], lsem.at[4 + i])
        for i, (low, n) in enumerate(cuts)
    ]
    for load in (loads[2], loads[3], loads[0], *loads[4:], loads[1]):
        load.start()

    barrier = pltpu.get_barrier_semaphore()
    zz = p * 2 + zl
    greeted = [at(c=peer)]
    for o in range(1, 8):
        other = (zz + o) % 8
        greeted.append(at(zl=other % 2, p=other // 2))
        greeted.append(at(zl=other % 2, p=other // 2, c=peer))
    for o in range(1, 4):
        greeted.append(at(x=(x + o) % 4))
        greeted.append(at(y=(y + o) % 4))
    for device in greeted:
        pl.semaphore_signal(barrier, inc=1, device_id=device, device_id_type=MESH)

    spot = lax.broadcasted_iota(jnp.int32, (400, WIDE), 1)
    sel = (spot == lax.broadcasted_iota(jnp.int32, (400, WIDE), 0) + 16 * t).astype(BF16)
    hw[0] = jnp.zeros((64, WIDE), BF16)
    hw[9] = jnp.zeros((64, WIDE), BF16)
    for j in range(25):
        lsrow[:, j * 128 : (j + 1) * 128] = ls_ref[j : j + 1, :]

    def block_of(k):
        return jnp.where(k == 0, p2, jnp.where(k == 1, p1, jnp.where(k == 2, p3, p)))

    def teacher_half(k, h):
        columns = pl.ds(pl.multiple_of(STEP * h, 128), HALF)
        part[...] = (
            jnp.dot(hq[k], w[:, columns], preferred_element_type=F32) * lsrow[:, columns]
        )

        @pl.when(t // 4 == h)
        def _():
            window = pl.ds(pl.multiple_of(384 * (t % 4), 128), WIDE)
            part[:, window] += wide(rq[k])

        @pl.when((t == 3) & (h == 1))
        def _():
            part[:, 0:128] += wide(rq[k, :, 384:512])

        @pl.when((t == 4) & (h == 0))
        def _():
            part[:, STEP:HALF] += wide(rq[k, :, 0:128])

    def teacher_peer(k):
        tokens = pl.ds(pl.multiple_of(block_of(k) * 256, 256), 256)
        hq[k] = jnp.transpose(hid[:, tokens])
        rq[k] = across(res[:, tokens], sel).astype(BF16)
        teacher_half(k, peer)
        cs[k] = part[...].astype(BF16)

    loads[2].wait()
    htwo[...] = across(hrow[...], sel)
    hw[1 + t] = htwo[pl.ds(pl.multiple_of(row_block % 2 * 64, 64), 64), :].astype(BF16)

    pl.semaphore_wait(barrier, len(greeted))

    core_id = ids(4)

    def core_copy(k):
        return remote(cs.at[k], cr.at[k], core_id + k, at(c=peer))

    x_id = ids(1)

    def x_copy():
        return remote(xs.at[c], xs.at[c], x_id, at(c=peer))

    loads[3].wait()
    x_copy().start()

    hz_id = ids(3)

    def hz_copy(o):
        return remote(hw.at[1 + t], hw.at[1 + t], hz_id + o - 1, at(p=(p + o) % 4))

    for o in (1, 3, 2):
        hz_copy(o).start()

    hc_id = ids(4)

    def hc_copy(o):
        slot = 1 + 2 * ((p + 4 - o) % 4) + c
        return remote(hw.at[slot], hw.at[slot], hc_id + o, at(c=peer))

    h1_id = ids(6)

    def h1_copy(m, o):
        block = hd.at[x, y, :, pl.ds(896 * m, 896 - 128 * m)]
        device = at(x=(x + o) % 4) if m == 0 else at(y=(y + o) % 4)
        return remote(block, block, h1_id + 3 * m + o - 1, device)

    h2_id = ids(8)

    def h2_copy(m, n):
        a = y if m == 0 else x
        ahead, behind = (a + 1) % 4, (a + 3) % 4
        group = a if n < 2 else behind if n == 2 else ahead
        inner = pl.ds(0, 4) if n < 2 else pl.ds(2 * (n - 2), 2)
        to = ahead if n in (0, 2) else behind
        if m == 0:
            block, device = hd.at[inner, group, :, pl.ds(0, 896)], at(y=to)
        else:
            block, device = hd.at[group, inner, :, pl.ds(896, 768)], at(x=to)
        return remote(block, block, h2_id + 4 * m + n, device)

    def head_first():
        for o in range(4):
            if o:
                hz_copy(o).wait_recv()
            hc_copy(o).start()
        for o in range(4):
            hc_copy(o).wait_recv()
        for j in range(13):
            tile = hw[1 + 4 * c + j // 3, :, (j % 3) * 128 : (j % 3) * 128 + 128]
            if j % 3 == 0:
                tile = tile + hw[4 * c + j // 3, :, 384:512]
            hd[x, y, :, j * 128 : (j + 1) * 128] = tile
        for o in (1, 3, 2):
            for m in range(2):
                h1_copy(m, o).start()

    def head_second():
        for o in range(1, 4):
            for m in range(2):
                h1_copy(m, o).wait_recv()
        for n in range(2):
            for m in range(2):
                h2_copy(m, n).start()

    def head_third():
        for n in range(2):
            for m in range(2):
                h2_copy(m, n).wait_recv()
                h2_copy(m, n + 2).start()

    loads[0].wait()
    loads[1].wait()
    for load in loads[4:]:
        load.wait()
    teacher_peer(0)
    core_copy(0).start()

    a_id, b_id = ids(3 * CH), ids(3 * CH)
    rows = 128 // CH

    def a_copy(slot, piece):
        own = pl.ds(piece * rows, rows)
        src = fa.at[own] if slot == 2 else zs.at[slot, own]
        return remote(src, ra.at[slot, own], a_id + slot * CH + piece, at(p=p1))

    def b_copy(slot, piece):
        own = pl.ds(piece * rows, rows)
        src = fb.at[own] if slot == 2 else zs.at[2 * slot, pl.ds(128 + piece * rows, rows)]
        return remote(src, rb.at[slot, own], b_id + slot * CH + piece, at(p=p3))

    def teacher_step(k, carry):
        teacher_half(k, c)

        core_copy(k).wait_recv()
        zs[k] = (part[...] + wide(cr[k])).astype(BF16)

        @pl.when(k == 0)
        def _():
            for piece in range(CH):
                a_copy(0, piece).start()
                b_copy(0, piece).start()

        @pl.when(k == 1)
        def _():
            for piece in range(CH):
                a_copy(1, piece).start()

        @pl.when(k < 3)
        def _():
            teacher_peer(k + 1)
            core_copy(k + 1).start()

        @pl.when(k == 0)
        def _():
            head_first()

        @pl.when(k == 2)
        def _():
            head_second()

        return carry

    lax.fori_loop(0, 4, teacher_step, 0)

    def normalize(values):
        centered = values - jnp.mean(values, axis=1, keepdims=True)
        inverse = lax.rsqrt(jnp.mean(centered * centered, axis=1, keepdims=True) + epsilon)
        return centered * inverse, inverse

    x_copy().wait_recv()
    for h in range(2):
        normed, _ = normalize(wide(xs[h]))
        out = (normed * gain_ref[...]).astype(BF16)
        nb[h * 128 : (h + 1) * 128, :] = out
        turned = jnp.transpose(wide(out)).astype(BF16)
        nt[:, :, :, :, h * 128 : (h + 1) * 128] = turned.reshape(2, 4, 4, 32, 128)

    def piece_of(piece, first=0):
        return pl.ds(pl.multiple_of(first + piece * rows, rows), rows)

    def second_step(piece, carry):
        own = piece_of(piece)
        a_copy(0, piece).wait_recv()
        fb[own, :] = (wide(zs[2, own, :]) + wide(ra[0, own, :])).astype(BF16)
        b_copy(2, piece).start()
        b_copy(0, piece).wait_recv()
        fa[own, :] = (wide(zs[1, piece_of(piece, 128), :]) + wide(rb[0, own, :])).astype(BF16)
        a_copy(2, piece).start()
        return carry

    lax.fori_loop(0, CH, second_step, 0)
    head_third()
    for piece in range(CH):
        b_copy(1, piece).start()

    for m in range(2):
        for n in (2, 3):
            h2_copy(m, n).wait_recv()
    head = hd[...].reshape(1024, HALF)

    def predict(h, carry):
        block = pl.ds(pl.multiple_of(h * 128, 128), 128)
        pr[block, :] = jnp.dot(nb[block, :], head, preferred_element_type=F32)
        squares[block, :] = jnp.broadcast_to(
            jnp.sum(pr[block, :] * pr[block, :] * mine, axis=1, keepdims=True), (128, 128)
        )
        return carry

    lane = lax.broadcasted_iota(jnp.int32, (1, HALF), 1)
    mine = (lane >= 128 * c).astype(F32)
    small = lax.broadcasted_iota(jnp.int32, (rows, 128), 1)

    stat_id = ids(2 * CH)

    def stat_copy(h, piece):
        own = pl.ds(piece * rows, rows)
        return remote(st.at[h, own], sr.at[h, own], stat_id + h * CH + piece, at(c=peer))

    lax.fori_loop(0, 2, predict, 0)

    def finish(h):
        one, two = (ra, rb) if h == 0 else (rb, ra)

        def sums(piece, carry):
            (a_copy if h == 0 else b_copy)(1, piece).wait_recv()
            (b_copy if h == 0 else a_copy)(2, piece).wait_recv()
            own, block = piece_of(piece), piece_of(piece, h * 128)
            total = wide(zs[3, block, :]) + wide(one[1, own, :]) + wide(two[2, own, :])
            target = total.astype(BF16)
            tg[block, :] = target
            target = wide(target)
            masked = target * mine
            inner = jnp.sum(masked * pr[block, :], axis=1, keepdims=True)
            aim = jnp.sum(masked * target, axis=1, keepdims=True)
            st[h, own, :] = jnp.where(
                small == 0, inner, jnp.where(small == 1, squares[block, :], aim)
            )
            stat_copy(h, piece).start()
            return carry

        def grads(piece, carry):
            own, block = piece_of(piece), piece_of(piece, h * 128)
            stat_copy(h, piece).wait_recv()
            both = st[h, own, :] + sr[h, own, :]
            inner, square, aim = both[:, 0:1], both[:, 1:2], both[:, 2:3]
            scaling = lax.rsqrt((square + epsilon) * (aim + epsilon))
            cosine = inner * scaling
            pg[block, :] = (
                (cosine / (square + epsilon)) * pr[block, :] - scaling * wide(tg[block, :])
            ).astype(BF16)
            losses[own, :] = jnp.broadcast_to(1.0 - cosine, (rows, 128))
            return carry

        lax.fori_loop(0, CH, sums, 0)
        lax.fori_loop(0, CH, grads, 0)

        @pl.when(c == h)
        def _():
            loss_ref[...] = jnp.transpose(losses[...])[0:1, :]

    def back(h):
        grad = pg[h * 128 : (h + 1) * 128, :] * mine.astype(BF16)

        def one(q, carry):
            bp[h, :, pl.ds(pl.multiple_of(q * 256, 256), 256)] = lax.dot_general(
                grad, hd[q].reshape(256, HALF), (((1,), (1,)), ((), ())),
                preferred_element_type=F32,
            )
            return carry

        lax.fori_loop(0, 4, one, 0)

    finish(0)
    back(0)
    finish(1)

    parts = (pl.ds(0, 896), pl.ds(896, 768))
    gs, r1, f1, s1, r2 = (gs0, gs1), (r10, r11), (f10, f11), (s10, s11), (r20, r21)
    g_id = ids(24)
    axes = []
    for m in range(2):
        a = x if m == 0 else y
        axes.append((a, a + 1 - 2 * (a % 2), (a + 2) % 4, 3 - a))

    def g_copy(n, m, way, slot):
        a, near, far, last = axes[m]
        to = near if way == 0 else last
        device = at(x=to) if m == 0 else at(y=to)
        if slot == 2:
            src = f1[n].at[m, way]
        else:
            src = gs[n].at[m, far if slot == 0 else to, pl.ds(2 * way, 2)]
        dst = r1[n].at[m, way, slot]
        return remote(src, dst, g_id + n * 12 + m * 6 + way * 3 + slot, device)

    def gradient(n, send):
        def turn(j, carry):
            ax, ay = [
                jnp.where(j == 0, far, jnp.where(j == 1, near, jnp.where(j == 2, last, a)))
                for a, near, far, last in axes
            ]
            left = jnp.concatenate(
                [nt[0, ax].reshape(128, 256), nt[1, :, ay].reshape(128, 256)], axis=0
            )
            both = jnp.dot(left, pg[:, parts[n]], preferred_element_type=F32).astype(BF16)
            gs[n][0, ax] = both[0:128].reshape(4, 32, -1)
            gs[n][1, ay] = both[128:256].reshape(4, 32, -1)
            if send:

                @pl.when(j == 0)
                def _():
                    first_sends(n, 0)

                @pl.when(j == 2)
                def _():
                    first_sends(n, 1)

            return carry

        lax.fori_loop(0, 4, turn, 0)

    def first_sends(n, slot):
        for m in range(2):
            for way in range(2):
                g_copy(n, m, way, slot).start()

    def forward(n):
        for m in range(2):
            a, near, far, last = axes[m]
            for way in range(2):
                g_copy(n, m, 1 - way, 0).wait_recv()
                target, inner = (near, slice(2, 4)) if way == 0 else (last, slice(0, 2))
                f1[n][m, way] = (
                    wide(gs[n][m, target, inner])
                    + wide(r1[n][m, 1 - way, 0])
                ).astype(BF16)
                g_copy(n, m, way, 2).start()

    g2_id = ids(12)

    def g2_copy(n, m, o):
        b = y if m == 0 else x
        to = (b + o) % 4
        device = at(y=to) if m == 0 else at(x=to)
        return remote(
            s1[n].at[m, to], r2[n].at[m, o - 1],
            g2_id + 6 * n + 3 * m + o - 1, device,
        )

    def second_sends(n):
        for m in range(2):
            a = axes[m][0]
            for slot in (1, 2):
                for way in range(2):
                    g_copy(n, m, way, slot).wait_recv()
            for way in range(2):
                inner = slice(2 * way, 2 * way + 2)
                s1[n][m, inner] = (
                    wide(gs[n][m, a, inner])
                    + wide(r1[n][m, way, 1])
                    + wide(r1[n][m, 1 - way, 2])
                ).astype(BF16)
            for o in (1, 3, 2):
                g2_copy(n, m, o).start()

    def second_sums(n):
        for m in range(2):
            total = wide(s1[n][m, axes[1 - m][0]])
            for o in range(1, 4):
                g2_copy(n, m, o).wait_recv()
                total = total + wide(r2[n][m, o - 1])
            s2[m, :, parts[n]] = total.astype(BF16)

    g3_id = ids(16)

    def window_of(chip, core):
        return pl.ds(pl.multiple_of(768 * (chip % 2) + 384 * core, 128), WIDE)

    def g3_copy(o, core):
        to = (zz + o) % 8
        src = s2.at[to % 2, :, window_of(to // 2, core)]
        return remote(src, rz.at[o], g3_id + 2 * o + core, at(zl=to % 2, p=to // 2, c=core))

    def third(n, act):
        for o in (0, 1, 7, 2, 6, 3, 5, 4):
            chip = ((zz + o) % 8) // 2

            @pl.when((chip // 2 == c) & (chip % 2 == n))
            def _():
                if o:
                    act(g3_copy(o, c))
                act(g3_copy(o, peer))

    def third_sends(n):
        third(n, lambda copy: copy.start())

    gradient(0, True)
    gradient(1, False)
    forward(0)
    first_sends(1, 0)
    first_sends(1, 1)

    back(1)
    back_id = ids(1)

    def back_copy():
        return remote(bp.at[peer], br, back_id, at(c=peer))

    back_copy().start()
    second_sends(0)
    forward(1)

    second_sums(0)
    third_sends(0)
    second_sends(1)
    second_sums(1)
    third_sends(1)

    back_copy().wait_recv()
    normed, inverse = normalize(wide(xs[c]))
    normed_grad = (bp[c] + br[...]) * gain_ref[...]
    igrad_ref[...] = (
        inverse
        * (
            normed_grad
            - jnp.mean(normed_grad, axis=1, keepdims=True)
            - normed * jnp.mean(normed_grad * normed, axis=1, keepdims=True)
        )
    ).astype(BF16)

    @pl.when(p // 2 == c)
    def _():
        rz[0] = s2[zl, :, window_of(p, c)]

    @pl.when(p // 2 != c)
    def _():
        g3_copy(0, c).wait_recv()

    total = wide(rz[0])
    for o in range(1, 8):
        g3_copy(o, c).wait_recv()
        total = total + wide(rz[o])
    hgrad_ref[...] = total.astype(BF16)

    x_copy().wait_send()
    for o in range(1, 4):
        hz_copy(o).wait_send()
        for m in range(2):
            h1_copy(m, o).wait_send()
            for n in range(2):
                g2_copy(n, m, o).wait_send()
    for o in range(4):
        hc_copy(o).wait_send()
        for m in range(2):
            h2_copy(m, o).wait_send()
        core_copy(o).wait_send()
    for slot in range(3):
        for piece in range(CH):
            a_copy(slot, piece).wait_send()
            b_copy(slot, piece).wait_send()
        for m in range(2):
            for way in range(2):
                for n in range(2):
                    g_copy(n, m, way, slot).wait_send()
    for h in range(2):
        for piece in range(CH):
            stat_copy(h, piece).wait_send()
    back_copy().wait_send()
    for n in range(2):
        third(n, lambda copy: copy.wait_send())


def place(loss_ref, igrad_ref, hgrad_ref, loss_out, igrad_out, hgrad_out):
    loss_out[...] = loss_ref[...]
    igrad_out[...] = igrad_ref[...]
    t = lax.axis_index("tensor")
    first = 32 * (t // 2) + 16 * (t % 2)
    row = lax.broadcasted_iota(jnp.int32, (WIDE, 400), 0)
    pick = (row == lax.broadcasted_iota(jnp.int32, (WIDE, 400), 1) + first).astype(BF16)
    hgrad_out[...] = jnp.dot(hgrad_ref[...], pick, preferred_element_type=F32).astype(BF16)


def shards(
    teacher_hidden, down_weight, teacher_resid, layer_scale, student_x, norm_gain, head_weight
):
    hbm = pl.BlockSpec(memory_space=pl.ANY)
    vmem = pl.BlockSpec(memory_space=pltpu.VMEM)
    scratch = [
        ((800, 1024), BF16),
        ((4, 256, 800), BF16),
        ((4, 256, WIDE), BF16),
        ((800, DT), BF16),
        ((400, 1024), BF16),
        ((400, 128), BF16),
        ((128, WIDE), F32),
        ((1, DT), F32),
        ((256, HALF), F32),
        ((4, 256, HALF), BF16),
        ((4, 256, HALF), BF16),
        ((4, 256, HALF), BF16),
        ((3, 128, HALF), BF16),
        ((3, 128, HALF), BF16),
        ((128, HALF), BF16),
        ((128, HALF), BF16),
        ((10, 64, WIDE), BF16),
        ((4, 4, 64, HALF), BF16),
        ((2, 128, 1024), BF16),
        ((256, 1024), BF16),
        ((2, 4, 4, 32, 256), BF16),
        ((256, HALF), F32),
        ((256, HALF), BF16),
        ((256, 128), F32),
        ((256, HALF), BF16),
        ((128, 128), F32),
        ((2, 128, 128), F32),
        ((2, 128, 128), F32),
        ((2, 128, 1024), F32),
        ((128, 1024), F32),
        ((2, 4, 4, 32, 896), BF16),
        ((2, 4, 4, 32, 768), BF16),
        ((2, 2, 3, 2, 32, 896), BF16),
        ((2, 2, 3, 2, 32, 768), BF16),
        ((2, 2, 2, 32, 896), BF16),
        ((2, 2, 2, 32, 768), BF16),
        ((2, 4, 32, 896), BF16),
        ((2, 4, 32, 768), BF16),
        ((2, 3, 32, 896), BF16),
        ((2, 3, 32, 768), BF16),
        ((2, 32, HALF), BF16),
        ((8, 32, WIDE), BF16),
    ]
    copies = 1 + 3 + 4 + 6 + 8 + 4 + 6 * CH + 2 * CH + 24 + 12 + 16 + 1
    loss, input_grad, head_grad = pl.pallas_call(
        kernel,
        name="distill",
        out_shape=(
            jax.ShapeDtypeStruct((1, 128), F32),
            jax.ShapeDtypeStruct((128, 1024), BF16),
            jax.ShapeDtypeStruct((32, WIDE), BF16),
        ),
        in_specs=[hbm, hbm, hbm, vmem, hbm, vmem, hbm],
        out_specs=(vmem, vmem, vmem),
        scratch_shapes=[pltpu.VMEM(shape, kind) for shape, kind in scratch]
        + [
            pltpu.SemaphoreType.DMA((8,)),
            pltpu.SemaphoreType.DMA((copies,)),
            pltpu.SemaphoreType.DMA((copies,)),
        ],
        compiler_params=pltpu.CompilerParams(
            collective_id=0, has_side_effects=True, vmem_limit_bytes=60 * 2**20
        ),
        cost_estimate=pl.CostEstimate(
            flops=8_000_000_000, bytes_accessed=10_000_000, transcendentals=1000
        ),
    )(
        teacher_hidden.T,
        down_weight,
        teacher_resid.T,
        layer_scale.reshape(25, 128),
        student_x,
        norm_gain.reshape(1, -1),
        head_weight.T,
    )
    loss, input_grad, head_grad = pl.pallas_call(
        place,
        name="place",
        out_shape=(
            jax.ShapeDtypeStruct((1, 128), F32),
            jax.ShapeDtypeStruct((128, 1024), BF16),
            jax.ShapeDtypeStruct((32, 400), BF16),
        ),
        in_specs=[vmem, vmem, vmem],
        out_specs=(vmem, vmem, vmem),
    )(loss, input_grad, head_grad)
    return (loss.reshape(-1), input_grad, head_grad)


def solution(mesh):
    placed = (
        P("dp", "tensor"),
        P("tensor", None),
        P("dp", "tensor"),
        P(),
        P(("dp", "tensor"), None),
        P(),
        P(None, "tensor"),
    )
    return jax.shard_map(
        shards,
        mesh=mesh,
        in_specs=placed,
        out_specs=(P(("dp", "tensor")), P(("dp", "tensor"), None), P("dp", "tensor")),
        check_vma=False,
    )
```
